32 devices in a mesh: groups: 2 (over y), bank: 8 (over z, x), clus: 2 (over core).
Axes of the slice: x: 2, y: 2, z: 4, core: 2. Of those that a mesh axis runs over, the one named last changes fastest.
Arguments:
- features: bfloat16 [6144, 768], P(('groups', 'bank'), 'clus'), parts along dimension 0, may hold values from -6 to 6
- cluster_ids: int32 [6144], P(('groups', 'bank')), parts along dimension 0, may hold values from 0 to 4095, as said below
- w_in: bfloat16 [768, 1536], P(None, 'clus'), may hold values from -0.21875 to 0.21875
- w_out: bfloat16 [1536, 768], P('clus'), may hold values from -0.15625 to 0.15625
- old_centroids: bfloat16 [8192, 768], P(('groups', 'bank'), 'clus'), parts along dimension 0, may hold values from -6 to 6
Outputs:
- centroids: bfloat16 [8192, 768], P(('groups', 'bank')), parts along dimension 0
The draws below stay inside these ranges and needn't reach their ends.
There are 2 independent parts, one for each index of `groups`. The reference program is written for one: setup_inputs(seed, part) draws one part's arguments, and reference() takes and returns one part's arrays. A program takes and returns all parts, laid end to end along the dimension named above; an argument that names none is the same for every part. Nothing has to cross between parts.
Inputs may be any that keep to these rules, and one draw needn't show every extreme that they name: `cluster_ids`: cluster k is owned by bank index k // 512. The rows of one bank index name clusters of one owner at most 144 times, and one owner, drawn from the seed, receives exactly 144 rows from every bank index.
All inputs are finite; a program needn't handle non-finite values.
Results may differ from the reference program's by a relative error of at most 0.0035.
Values may be sent and summed in bfloat16 or wider, within the bound.
A program may use at most 64 MiB of HBM per device.

```python
import jax
import jax.numpy as jnp
from jax import lax

D = 768
HIDDEN_UNITS = 1536
ROWS = 384
CL_DEV = 512
CLUSTERS = 4096
ROWS_ALL = 3072
N_BANK = 8


def draw_cluster_ids(key, part):
    key = jax.random.fold_in(key, 7)
    hot_owner = jax.random.randint(jax.random.fold_in(key, 1), (), 0, N_BANK)
    capacity = 3 * ROWS // N_BANK
    others_count = ROWS - capacity
    per_owner = (others_count + N_BANK - 2) // (N_BANK - 1)

    def one_block(block_key):
        first_key, second_key, third_key = jax.random.split(block_key, 3)
        pool = jax.random.permutation(first_key, (N_BANK - 1) * per_owner)[:others_count] // per_owner
        others = pool + (pool >= hot_owner).astype(jnp.int32)
        owners = jnp.concatenate([jnp.full((capacity,), hot_owner, jnp.int32), others.astype(jnp.int32)])
        owners = jax.random.permutation(second_key, owners)
        local_ids = jax.random.randint(third_key, (ROWS,), 0, CL_DEV)
        return owners * CL_DEV + local_ids
    block_keys = jax.random.split(jax.random.fold_in(key, 2), N_BANK)
    return jax.vmap(one_block)(block_keys).reshape(-1).astype(jnp.int32)


def block_scale(stream_key, shape, pieces, least, top_value):
    factor_of = 1.0
    for position, parts in pieces:
        draws = jax.random.uniform(jax.random.fold_in(jax.random.fold_in(stream_key, 6), position), (parts,), jnp.float32, least / len(pieces), top_value / len(pieces))
        factor_of = factor_of * jnp.repeat(jnp.exp(draws), shape[position] // parts).reshape((-1,) + (1,) * (len(shape) - 1 - position))
    return factor_of


def normal_values(key, dims, width, limit, cuts=(), held_as=jnp.bfloat16):
    array = jax.random.normal(key, dims, jnp.float32) * width
    if len(cuts) > 0:
        array = block_scale(key, dims, cuts, -0.22, 0.18) * array
    return jnp.clip(array, min=-limit, max=limit).astype(held_as)


def setup_inputs(seed: int = 0, part: int = 0) -> dict:
    keys = jax.random.split(jax.random.key(seed), 6)
    part_keys = jax.random.split(jax.random.fold_in(keys[5], part), 6)
    return {
        "features": normal_values(part_keys[0], (ROWS_ALL, D), 1.0, 6.0, ((0, 8), (1, 2))),
        "cluster_ids": draw_cluster_ids(jax.random.fold_in(jax.random.fold_in(keys[5], part), 71), part),
        "w_in": normal_values(keys[2], (D, HIDDEN_UNITS), D ** -0.5, 0.21875, ((1, 2),)),
        "w_out": normal_values(keys[3], (HIDDEN_UNITS, D), HIDDEN_UNITS ** -0.5, 0.15625, ((0, 2),)),
        "old_centroids": normal_values(part_keys[4], (CLUSTERS, D), 1.0, 6.0, ((0, 8), (1, 2))),
    }


epsilon = 1e-06

def reference(features, cluster_ids, w_in, w_out, old_centroids):
    blocks = features.reshape(N_BANK, ROWS, D)

    def encode(rows_in):
        hidden = jax.nn.gelu(jnp.dot(rows_in, w_in, preferred_element_type=jnp.float32)).astype(jnp.bfloat16)
        residual = rows_in.astype(jnp.float32) + jnp.dot(hidden, w_out, preferred_element_type=jnp.float32)
        scale = lax.rsqrt(lax.optimization_barrier(jnp.mean(residual * residual, axis=1, keepdims=True)) + epsilon)
        return (residual * scale).astype(jnp.bfloat16)
    row_keys = lax.map(encode, blocks).reshape(ROWS_ALL, D)
    cluster_sums = jax.ops.segment_sum(row_keys.astype(jnp.float32), cluster_ids, num_segments=CLUSTERS)
    counts = jax.ops.segment_sum(jnp.ones((ROWS_ALL,), jnp.float32), cluster_ids, num_segments=CLUSTERS)
    pooled = (cluster_sums + old_centroids.astype(jnp.float32)) / (counts[:, None] + 1.0)
    scale = lax.rsqrt(lax.optimization_barrier(jnp.mean(pooled * pooled, axis=1, keepdims=True)) + epsilon)
    return (pooled * scale).astype(jnp.bfloat16)
```

```python
import functools

import jax
import jax.numpy as jnp
from jax import lax
from jax.experimental import pallas as pl
from jax.experimental.pallas import tpu as pltpu
from jax.sharding import PartitionSpec as P

D = 768
epsilon = 1e-06
BF16 = jnp.bfloat16
F32 = jnp.float32
MESH = pl.DeviceIdType.MESH


def dot(a, b):
    return jnp.dot(a, b, preferred_element_type=F32)


def each(low, high, body):
    if high - low <= 8:
        for d in range(low, high):
            body(d)
    else:

        def step(d, carry):
            body(d)
            return carry

        lax.fori_loop(low, high, step, 0)


def kernel(
    n, n_rows, n_out, features_in, ids_ref, w_in_in, w_out_in, old_in, out_ref,
    features, peer, w_in, w_out, old, hidden_sum, part, part_send, part_recv,
    sq_send, sq_recv, keys, pick, stage, recv, ids_send, ids_recv, member, counts, sums,
    fin_send, fin_recv, fin_half, load_sems, pair_send, pair_recv, part_s, part_r,
    sq_s, sq_r, ids_s, ids_r, row_s, row_r, fin_s, fin_r, half_s, half_r, own_s,
):
    group = lax.axis_index("groups")
    me = lax.axis_index("bank")
    core = lax.axis_index("clus")
    rows, half = features.shape
    owned = sums.shape[0]
    slots = recv.shape[1]
    row_block = rows // n_rows
    out_block = owned // n_out
    other = (group, me, 1 - core)

    def bank(d):
        return (group, lax.rem(me + d, n), core)

    def remote(src, dst, send, arrive, to):
        return pltpu.make_async_remote_copy(
            src_ref=src, dst_ref=dst, send_sem=send, recv_sem=arrive,
            device_id=to, device_id_type=MESH,
        )

    barrier = pltpu.get_barrier_semaphore()
    pl.semaphore_signal(barrier, inc=1, device_id=other, device_id_type=MESH)
    each(
        1, n,
        lambda d: pl.semaphore_signal(barrier, inc=1, device_id=bank(d), device_id_type=MESH),
    )
    loads = [
        pltpu.make_async_copy(src, dst, load_sems.at[i])
        for i, (src, dst) in enumerate(
            ((features_in, features), (w_in_in, w_in), (w_out_in, w_out), (old_in, old))
        )
    ]
    for load in loads:
        load.start()

    ids = ids_ref[...]
    owner = lax.div(ids, jnp.int32(owned))
    local = ids - owner * owned + 1
    owner_rows = max(16, n)
    table = jnp.where(
        lax.broadcasted_iota(jnp.int32, (owner_rows, rows), 0) == owner, 1.0, 0.0
    )
    earlier = jnp.where(
        lax.broadcasted_iota(jnp.int32, (rows, rows), 0)
        < lax.broadcasted_iota(jnp.int32, (rows, rows), 1),
        1.0, 0.0,
    ).astype(BF16)
    before = dot(table.astype(BF16), earlier)
    rank = jnp.sum(before * table, axis=0, keepdims=True).astype(jnp.int32)
    high = lax.div(local, jnp.int32(32))
    low = local - 32 * high
    digits = jnp.where(
        lax.broadcasted_iota(jnp.int32, (16, rows), 0) < 8, high, low
    ).astype(F32).astype(BF16)

    def place(d):
        to = lax.rem(me + d, n)
        slot = jnp.where(owner == to, rank, -1)
        chosen = jnp.where(
            lax.broadcasted_iota(jnp.int32, (slots, rows), 0) == slot, 1.0, 0.0
        ).astype(BF16)
        pick[d] = chosen
        found = lax.dot_general(
            digits, chosen, (((1,), (1,)), ((), ())), preferred_element_type=F32
        )
        ids_send[d, :, :slots] = (32.0 * found[:8] + found[8:] - 1.0).astype(jnp.int32)

    each(0, n, place)

    pl.semaphore_wait(barrier, n)
    loads[0].wait()
    to_peer = remote(features, peer, pair_send, pair_recv, other)
    to_peer.start()

    def id_copy(d):
        return remote(ids_send.at[d], ids_recv.at[d], ids_s.at[d], ids_r.at[d], bank(d))

    each(1, n, lambda d: id_copy(d).start())

    mine = pl.ds(pl.multiple_of(core * half, 128), half)
    theirs = pl.ds(pl.multiple_of((1 - core) * half, 128), half)
    loads[1].wait()
    hidden_sum[...] = dot(features[...], w_in[mine, :])
    loads[2].wait()
    to_peer.wait()
    part_copies = []
    for b in range(n_rows):
        block = slice(b * row_block, (b + 1) * row_block)
        hidden = jax.nn.gelu(
            hidden_sum[block, :] + dot(peer[block, :], w_in[theirs, :])
        ).astype(BF16)
        part_send[block, :] = dot(hidden, w_out[:, theirs])
        copy = remote(part_send.at[block], part_recv.at[block], part_s.at[b], part_r.at[b], other)
        copy.start()
        part_copies.append(copy)
        part[block, :] = features[block, :].astype(F32) + dot(hidden, w_out[:, mine])

    sq_copies = []
    for b in range(n_rows):
        block = slice(b * row_block, (b + 1) * row_block)
        part_copies[b].wait()
        residual = part[block, :] + part_recv[block, :]
        part[block, :] = residual
        sq_send[block, :] = jnp.broadcast_to(
            jnp.sum(residual * residual, axis=1, keepdims=True), (row_block, 128)
        )
        copy = remote(sq_send.at[block], sq_recv.at[block], sq_s.at[b], sq_r.at[b], other)
        copy.start()
        sq_copies.append(copy)
    for b in range(n_rows):
        block = slice(b * row_block, (b + 1) * row_block)
        sq_copies[b].wait()
        total = sq_send[block, :1] + sq_recv[block, :1]
        keys[block, :] = (part[block, :] * lax.rsqrt(total / D + epsilon)).astype(BF16)

    def row_copy(d):
        return remote(stage.at[d], recv.at[d], row_s.at[d], row_r.at[d], bank(d))

    def dispatch(d):
        stage[d] = dot(pick[d], keys[...]).astype(BF16)
        row_copy(d).start()

    each(1, n, dispatch)
    stage[0] = dot(pick[0], keys[...]).astype(BF16)

    def members(cluster_ids):
        found = jnp.where(
            lax.broadcasted_iota(jnp.int32, (owned, slots), 0) == cluster_ids, 1.0, 0.0
        )
        return found.astype(BF16), jnp.sum(found, axis=1, keepdims=True)

    own_member, own_count = members(ids_send[0, :1, :slots])
    counts[...] = jnp.broadcast_to(own_count, counts.shape)
    sums[...] = dot(own_member, stage[0])

    def match(d):
        id_copy(d).wait()
        chosen, count = members(ids_recv[d, :1, :slots])
        member[d] = chosen
        counts[...] += count

    each(1, n, match)
    loads[3].wait()

    def collect(d):
        row_copy(d).wait()
        sums[...] += dot(member[d], recv[d])

    each(1, n, collect)

    fin_copies = []
    for b in range(n_out):
        block = slice(b * out_block, (b + 1) * out_block)
        pooled = (sums[block, :] + old[block, :].astype(F32)) / (counts[block, :1] + 1.0)
        sums[block, :] = pooled
        fin_send[block, :] = jnp.broadcast_to(
            jnp.sum(pooled * pooled, axis=1, keepdims=True), (out_block, 128)
        )
        copy = remote(fin_send.at[block], fin_recv.at[block], fin_s.at[b], fin_r.at[b], other)
        copy.start()
        fin_copies.append(copy)
    half_copies = []
    for b in range(n_out):
        block = slice(b * out_block, (b + 1) * out_block)
        fin_copies[b].wait()
        total = fin_send[block, :1] + fin_recv[block, :1]
        fin_half[block, :] = (sums[block, :] * lax.rsqrt(total / D + epsilon)).astype(BF16)
        place_at = out_ref.at[block, mine]
        copy = remote(fin_half.at[block], place_at, half_s.at[b], half_r.at[b], other)
        copy.start()
        here = pltpu.make_async_copy(fin_half.at[block], place_at, own_s.at[b])
        here.start()
        half_copies += [copy, here]
    for copy in half_copies:
        copy.wait()


def shards(features, cluster_ids, w_in, w_out, old_centroids):
    n = lax.axis_size("bank")
    rows, half = features.shape
    hidden = w_in.shape[1]
    owned = old_centroids.shape[0]
    capacity = 3 * rows // n
    slots = -(-capacity // 16) * 16
    width = -(-slots // 128) * 128
    n_rows, n_out = 3, 4
    vmem, dma = pltpu.VMEM, pltpu.SemaphoreType.DMA
    anywhere = pl.BlockSpec(memory_space=pl.ANY)
    return pl.pallas_call(
        functools.partial(kernel, n, n_rows, n_out),
        out_shape=jax.ShapeDtypeStruct((owned, 2 * half), BF16),
        in_specs=[
            anywhere, pl.BlockSpec(memory_space=pltpu.VMEM), anywhere, anywhere, anywhere,
        ],
        out_specs=anywhere,
        scratch_shapes=[
            vmem((rows, half), BF16),
            vmem((rows, half), BF16),
            vmem(w_in.shape, BF16),
            vmem(w_out.shape, BF16),
            vmem((owned, half), BF16),
            vmem((rows, hidden), F32),
            vmem((rows, half), F32),
            vmem((rows, half), F32),
            vmem((rows, half), F32),
            vmem((rows, 128), F32),
            vmem((rows, 128), F32),
            vmem((rows, half), BF16),
            vmem((n, slots, rows), BF16),
            vmem((n, slots, half), BF16),
            vmem((n, slots, half), BF16),
            vmem((n, 8, width), jnp.int32),
            vmem((n, 8, width), jnp.int32),
            vmem((n, owned, slots), BF16),
            vmem((owned, 128), F32),
            vmem((owned, half), F32),
            vmem((owned, 128), F32),
            vmem((owned, 128), F32),
            vmem((owned, half), BF16),
            dma((4,)), dma, dma, dma((n_rows,)), dma((n_rows,)),
            dma((n_rows,)), dma((n_rows,)), dma((n,)), dma((n,)), dma((n,)), dma((n,)),
            dma((n_out,)), dma((n_out,)), dma((n_out,)), dma((n_out,)), dma((n_out,)),
        ],
        compiler_params=pltpu.CompilerParams(
            collective_id=0, has_side_effects=True, vmem_limit_bytes=50 * 1024 * 1024
        ),
    )(features, cluster_ids.reshape(1, rows), w_in, w_out, old_centroids)


def solution(mesh):
    placed = (
        P(("groups", "bank"), "clus"),
        P(("groups", "bank")),
        P(None, "clus"),
        P("clus", None),
        P(("groups", "bank"), "clus"),
    )
    return jax.shard_map(
        shards, mesh=mesh, in_specs=placed, out_specs=P(("groups", "bank"), None), check_vma=False
    )
```

```python
import functools

import jax
import jax.numpy as jnp
from jax import lax
from jax.experimental import pallas as pl
from jax.experimental.pallas import tpu as pltpu
from jax.sharding import PartitionSpec as P

D = 768
epsilon = 1e-06
BF16 = jnp.bfloat16
F32 = jnp.float32
MESH = pl.DeviceIdType.MESH


def dot(a, b):
    return jnp.dot(a, b, preferred_element_type=F32)


def each(low, high, body):
    if high - low <= 8:
        for d in range(low, high):
            body(d)
    else:

        def step(d, carry):
            body(d)
            return carry

        lax.fori_loop(low, high, step, 0)


def kernel(
    n, n_rows, n_out, features_in, ids_ref, w_in_in, w_out_in, old_in, out_ref,
    features, peer, w_in, w_out, old, hidden_sum, part, part_send, part_recv,
    sq_send, sq_recv, keys, pick, stage, recv, ids_send, ids_recv, member, counts, sums,
    fin_send, fin_recv, fin_half, load_sems, pair_send, pair_recv, part_s, part_r,
    sq_s, sq_r, ids_s, ids_r, row_s, row_r, fin_s, fin_r, half_s, half_r, own_s,
):
    group = lax.axis_index("groups")
    me = lax.axis_index("bank")
    core = lax.axis_index("clus")
    rows, half = features.shape
    owned = sums.shape[0]
    slots = recv.shape[1]
    row_block = rows // n_rows
    out_block = owned // n_out
    other = (group, me, 1 - core)

    def bank(d):
        return (group, lax.rem(me + d, n), core)

    def remote(src, dst, send, arrive, to):
        return pltpu.make_async_remote_copy(
            src_ref=src, dst_ref=dst, send_sem=send, recv_sem=arrive,
            device_id=to, device_id_type=MESH,
        )

    barrier = pltpu.get_barrier_semaphore()
    pl.semaphore_signal(barrier, inc=1, device_id=other, device_id_type=MESH)
    each(
        1, n,
        lambda d: pl.semaphore_signal(barrier, inc=1, device_id=bank(d), device_id_type=MESH),
    )
    loads = [
        pltpu.make_async_copy(src, dst, load_sems.at[i])
        for i, (src, dst) in enumerate(
            ((features_in, features), (w_in_in, w_in), (w_out_in, w_out), (old_in, old))
        )
    ]
    for load in loads:
        load.start()

    ids = ids_ref[...].reshape(1, rows)
    owner = lax.div(ids, jnp.int32(owned))
    local = ids - owner * owned + 1
    owner_rows = max(16, n)
    table = jnp.where(
        lax.broadcasted_iota(jnp.int32, (owner_rows, rows), 0) == owner, 1.0, 0.0
    )
    earlier = jnp.where(
        lax.broadcasted_iota(jnp.int32, (rows, rows), 0)
        < lax.broadcasted_iota(jnp.int32, (rows, rows), 1),
        1.0, 0.0,
    ).astype(BF16)
    before = dot(table.astype(BF16), earlier)
    rank = jnp.sum(before * table, axis=0, keepdims=True).astype(jnp.int32)
    high = lax.div(local, jnp.int32(32))
    low = local - 32 * high
    digits = jnp.where(
        lax.broadcasted_iota(jnp.int32, (16, rows), 0) < 8, high, low
    ).astype(F32).astype(BF16)

    def place(d):
        to = lax.rem(me + d, n)
        slot = jnp.where(owner == to, rank, -1)
        chosen = jnp.where(
            lax.broadcasted_iota(jnp.int32, (slots, rows), 0) == slot, 1.0, 0.0
        ).astype(BF16)
        pick[d] = chosen
        found = lax.dot_general(
            digits, chosen, (((1,), (1,)), ((), ())), preferred_element_type=F32
        )
        ids_send[d, :, :slots] = (32.0 * found[:8] + found[8:] - 1.0).astype(jnp.int32)

    each(0, n, place)

    pl.semaphore_wait(barrier, n)
    loads[0].wait()
    to_peer = remote(features, peer, pair_send, pair_recv, other)
    to_peer.start()

    def id_copy(d):
        return remote(ids_send.at[d], ids_recv.at[d], ids_s.at[d], ids_r.at[d], bank(d))

    each(1, n, lambda d: id_copy(d).start())

    mine = pl.ds(pl.multiple_of(core * half, 128), half)
    theirs = pl.ds(pl.multiple_of((1 - core) * half, 128), half)
    loads[1].wait()
    hidden_sum[...] = dot(features[...], w_in[mine, :])
    loads[2].wait()
    to_peer.wait()
    part_copies = []
    for b in range(n_rows):
        block = slice(b * row_block, (b + 1) * row_block)
        hidden = jax.nn.gelu(
            hidden_sum[block, :] + dot(peer[block, :], w_in[theirs, :])
        ).astype(BF16)
        part_send[block, :] = dot(hidden, w_out[:, theirs])
        copy = remote(part_send.at[block], part_recv.at[block], part_s.at[b], part_r.at[b], other)
        copy.start()
        part_copies.append(copy)
        part[block, :] = features[block, :].astype(F32) + dot(hidden, w_out[:, mine])

    sq_copies = []
    for b in range(n_rows):
        block = slice(b * row_block, (b + 1) * row_block)
        part_copies[b].wait()
        residual = part[block, :] + part_recv[block, :]
        part[block, :] = residual
        sq_send[block, :] = jnp.broadcast_to(
            jnp.sum(residual * residual, axis=1, keepdims=True), (row_block, 128)
        )
        copy = remote(sq_send.at[block], sq_recv.at[block], sq_s.at[b], sq_r.at[b], other)
        copy.start()
        sq_copies.append(copy)
    for b in range(n_rows):
        block = slice(b * row_block, (b + 1) * row_block)
        sq_copies[b].wait()
        total = sq_send[block, :1] + sq_recv[block, :1]
        keys[block, :] = (part[block, :] * lax.rsqrt(total / D + epsilon)).astype(BF16)

    def row_copy(d):
        return remote(stage.at[d], recv.at[d], row_s.at[d], row_r.at[d], bank(d))

    def dispatch(d):
        stage[d] = dot(pick[d], keys[...]).astype(BF16)
        row_copy(d).start()

    each(1, n, dispatch)
    stage[0] = dot(pick[0], keys[...]).astype(BF16)

    def members(cluster_ids):
        found = jnp.where(
            lax.broadcasted_iota(jnp.int32, (owned, slots), 0) == cluster_ids, 1.0, 0.0
        )
        return found.astype(BF16), jnp.sum(found, axis=1, keepdims=True)

    own_member, own_count = members(ids_send[0, :1, :slots])
    counts[...] = jnp.broadcast_to(own_count, counts.shape)
    sums[...] = dot(own_member, stage[0])

    def match(d):
        id_copy(d).wait()
        chosen, count = members(ids_recv[d, :1, :slots])
        member[d] = chosen
        counts[...] += count

    each(1, n, match)
    loads[3].wait()

    def collect(d):
        row_copy(d).wait()
        sums[...] += dot(member[d], recv[d])

    each(1, n, collect)

    fin_copies = []
    for b in range(n_out):
        block = slice(b * out_block, (b + 1) * out_block)
        pooled = (sums[block, :] + old[block, :].astype(F32)) / (counts[block, :1] + 1.0)
        sums[block, :] = pooled
        fin_send[block, :] = jnp.broadcast_to(
            jnp.sum(pooled * pooled, axis=1, keepdims=True), (out_block, 128)
        )
        copy = remote(fin_send.at[block], fin_recv.at[block], fin_s.at[b], fin_r.at[b], other)
        copy.start()
        fin_copies.append(copy)
    half_copies = []
    for b in range(n_out):
        block = slice(b * out_block, (b + 1) * out_block)
        fin_copies[b].wait()
        total = fin_send[block, :1] + fin_recv[block, :1]
        fin_half[block, :] = (sums[block, :] * lax.rsqrt(total / D + epsilon)).astype(BF16)
        place_at = out_ref.at[block, mine]
        copy = remote(fin_half.at[block], place_at, half_s.at[b], half_r.at[b], other)
        copy.start()
        here = pltpu.make_async_copy(fin_half.at[block], place_at, own_s.at[b])
        here.start()
        half_copies += [copy, here]
    for copy in half_copies:
        copy.wait()


def shards(features, cluster_ids, w_in, w_out, old_centroids):
    n = lax.axis_size("bank")
    rows, half = features.shape
    hidden = w_in.shape[1]
    owned = old_centroids.shape[0]
    capacity = 3 * rows // n
    slots = -(-capacity // 16) * 16
    width = -(-slots // 128) * 128
    n_rows, n_out = 3, 4
    vmem, dma = pltpu.VMEM, pltpu.SemaphoreType.DMA
    anywhere = pl.BlockSpec(memory_space=pl.ANY)
    far = pl.BlockSpec(memory_space=pltpu.HBM)
    return pl.pallas_call(
        functools.partial(kernel, n, n_rows, n_out),
        out_shape=jax.ShapeDtypeStruct((owned, 2 * half), BF16),
        in_specs=[
            far, pl.BlockSpec(memory_space=pltpu.VMEM), far, far, far,
        ],
        out_specs=anywhere,
        scratch_shapes=[
            vmem((rows, half), BF16),
            vmem((rows, half), BF16),
            vmem(w_in.shape, BF16),
            vmem(w_out.shape, BF16),
            vmem((owned, half), BF16),
            vmem((rows, hidden), F32),
            vmem((rows, half), F32),
            vmem((rows, half), F32),
            vmem((rows, half), F32),
            vmem((rows, 128), F32),
            vmem((rows, 128), F32),
            vmem((rows, half), BF16),
            vmem((n, slots, rows), BF16),
            vmem((n, slots, half), BF16),
            vmem((n, slots, half), BF16),
            vmem((n, 8, width), jnp.int32),
            vmem((n, 8, width), jnp.int32),
            vmem((n, owned, slots), BF16),
            vmem((owned, 128), F32),
            vmem((owned, half), F32),
            vmem((owned, 128), F32),
            vmem((owned, 128), F32),
            vmem((owned, half), BF16),
            dma((4,)), dma, dma, dma((n_rows,)), dma((n_rows,)),
            dma((n_rows,)), dma((n_rows,)), dma((n,)), dma((n,)), dma((n,)), dma((n,)),
            dma((n_out,)), dma((n_out,)), dma((n_out,)), dma((n_out,)), dma((n_out,)),
        ],
        compiler_params=pltpu.CompilerParams(
            collective_id=0, has_side_effects=True, vmem_limit_bytes=50 * 1024 * 1024
        ),
    )(
        pltpu.with_memory_space_constraint(features, pltpu.HBM),
        cluster_ids,
        pltpu.with_memory_space_constraint(w_in, pltpu.HBM),
        pltpu.with_memory_space_constraint(w_out, pltpu.HBM),
        pltpu.with_memory_space_constraint(old_centroids, pltpu.HBM),
    )


def solution(mesh):
    placed = (
        P(("groups", "bank"), "clus"),
        P(("groups", "bank")),
        P(None, "clus"),
        P("clus", None),
        P(("groups", "bank"), "clus"),
    )
    return jax.shard_map(
        shards, mesh=mesh, in_specs=placed, out_specs=P(("groups", "bank"), None), check_vma=False
    )
```

```python
import functools

import jax
import jax.numpy as jnp
from jax import lax
from jax.experimental import pallas as pl
from jax.experimental.pallas import tpu as pltpu
from jax.sharding import PartitionSpec as P

D = 768
epsilon = 1e-06
BF16 = jnp.bfloat16
F32 = jnp.float32
MESH = pl.DeviceIdType.MESH


def dot(a, b):
    return jnp.dot(a, b, preferred_element_type=F32)


def each(low, high, body):
    if high - low <= 8:
        for d in range(low, high):
            body(d)
    else:

        def step(d, carry):
            body(d)
            return carry

        lax.fori_loop(low, high, step, 0)


def kernel(
    n, n_rows, n_out, features_in, ids_ref, w_in_in, w_out_in, old_in, out_ref,
    features, peer, w_in, w_out, old, hidden_sum, hidden, part, part_send, part_recv,
    sq_send, sq_recv, keys, pick, stage_lead, recv_lead, stage, recv, ids_send, ids_recv, member, counts, sums, scale_send, scale_recv,
    fin_send, fin_recv, fin_half, load_sems, pair_send, pair_recv, part_s, part_r,
    sq_s, sq_r, ids_s, ids_r, lead_s, lead_r, scale_s, scale_r, row_s, row_r, fin_s, fin_r, half_s, half_r, own_s,
):
    group = lax.axis_index("groups")
    me = lax.axis_index("bank")
    core = lax.axis_index("clus")
    rows, half = features.shape
    owned = sums.shape[0]
    slots = recv.shape[1]
    row_block = rows // n_rows
    out_block = owned // n_out
    other = (group, me, 1 - core)

    def bank(d):
        return (group, lax.rem(me + d, n), core)

    def remote(src, dst, send, arrive, to):
        return pltpu.make_async_remote_copy(
            src_ref=src, dst_ref=dst, send_sem=send, recv_sem=arrive,
            device_id=to, device_id_type=MESH,
        )

    barrier = pltpu.get_barrier_semaphore()
    pl.semaphore_signal(barrier, inc=1, device_id=other, device_id_type=MESH)
    each(
        1, n,
        lambda d: pl.semaphore_signal(barrier, inc=1, device_id=bank(d), device_id_type=MESH),
    )
    loads = [
        pltpu.make_async_copy(src, dst, load_sems.at[i])
        for i, (src, dst) in enumerate(
            ((features_in, features), (w_in_in, w_in), (w_out_in, w_out), (old_in, old))
        )
    ]
    for load in loads:
        load.start()

    ids = ids_ref[...].reshape(1, rows)
    owner = lax.div(ids, jnp.int32(owned))
    local = ids - owner * owned + 1
    owner_rows = max(16, n)
    table = jnp.where(
        lax.broadcasted_iota(jnp.int32, (owner_rows, rows), 0) == owner, 1.0, 0.0
    )
    earlier = jnp.where(
        lax.broadcasted_iota(jnp.int32, (rows, rows), 0)
        < lax.broadcasted_iota(jnp.int32, (rows, rows), 1),
        1.0, 0.0,
    ).astype(BF16)
    before = dot(table.astype(BF16), earlier)
    rank = jnp.sum(before * table, axis=0, keepdims=True).astype(jnp.int32)
    high = lax.div(local, jnp.int32(32))
    low = local - 32 * high
    digits = jnp.where(
        lax.broadcasted_iota(jnp.int32, (16, rows), 0) < 8, high, low
    ).astype(F32).astype(BF16)

    def place(d):
        to = lax.rem(me + d, n)
        slot = jnp.where(owner == to, rank, -1)
        chosen = jnp.where(
            lax.broadcasted_iota(jnp.int32, (slots, rows), 0) == slot, 1.0, 0.0
        ).astype(BF16)
        pick[d] = chosen
        found = lax.dot_general(
            digits, chosen, (((1,), (1,)), ((), ())), preferred_element_type=F32
        )
        ids_send[d, :, :slots] = (32.0 * found[:8] + found[8:] - 1.0).astype(jnp.int32)

    each(0, n, place)

    pl.semaphore_wait(barrier, n)
    loads[0].wait()
    to_peer = remote(features, peer, pair_send, pair_recv, other)
    to_peer.start()

    def id_copy(d):
        return remote(ids_send.at[d], ids_recv.at[d], ids_s.at[d], ids_r.at[d], bank(d))

    each(1, n, lambda d: id_copy(d).start())

    mine = pl.ds(pl.multiple_of(core * half, 128), half)
    theirs = pl.ds(pl.multiple_of((1 - core) * half, 128), half)
    loads[1].wait()
    hidden_sum[...] = dot(features[...], w_in[mine, :])
    loads[2].wait()
    to_peer.wait()
    lead = recv_lead.shape[2]
    front, back = slice(0, lead), slice(lead, half)

    def columns(first, width, own):
        base = core if own else 1 - core
        return pl.ds(pl.multiple_of(base * half + first, 128), width)

    lead_copies = []
    for b in range(n_rows):
        block = slice(b * row_block, (b + 1) * row_block)
        hidden[block, :] = jax.nn.gelu(
            hidden_sum[block, :] + dot(peer[block, :], w_in[theirs, :])
        ).astype(BF16)
        part_send[block, front] = dot(hidden[block, :], w_out[:, columns(0, lead, False)])
        copy = remote(
            part_send.at[block, front], part_recv.at[block, front],
            part_s.at[b], part_r.at[b], other,
        )
        copy.start()
        lead_copies.append(copy)
    part_send[:, back] = dot(hidden[...], w_out[:, columns(lead, half - lead, False)])
    rest_copy = remote(
        part_send.at[:, back], part_recv.at[:, back],
        part_s.at[n_rows], part_r.at[n_rows], other,
    )
    rest_copy.start()
    part[:, front] = features[:, front].astype(F32) + dot(
        hidden[...], w_out[:, columns(0, lead, True)]
    )
    for copy in lead_copies:
        copy.wait()
    lead_residual = part[:, front] + part_recv[:, front]
    keys[:, front] = lead_residual.astype(BF16)

    def lead_rows(d):
        return remote(
            stage_lead.at[d], recv_lead.at[d], lead_s.at[d], lead_r.at[d], bank(d)
        )

    def dispatch_lead(d):
        stage_lead[d] = dot(pick[d], keys[:, front]).astype(BF16)
        lead_rows(d).start()

    each(1, n, dispatch_lead)

    part[:, back] = features[:, back].astype(F32) + dot(
        hidden[...], w_out[:, columns(lead, half - lead, True)]
    )
    lead_squares = jnp.sum(lead_residual * lead_residual, axis=1, keepdims=True)
    rest_copy.wait()
    residual = part[:, back] + part_recv[:, back]
    part[:, back] = residual
    squares = lead_squares + jnp.sum(residual * residual, axis=1, keepdims=True)
    sq_send[...] = jnp.transpose(jnp.broadcast_to(squares, (rows, 128)))[:8]
    sq_copy = remote(sq_send, sq_recv, sq_s, sq_r, other)
    sq_copy.start()
    sq_copy.wait()
    scale = lax.rsqrt((sq_send[...] + sq_recv[...]) / D + epsilon)
    column = jnp.transpose(jnp.broadcast_to(scale[:1], (128, rows)))[:, :1]
    keys[:, back] = (part[:, back] * column).astype(BF16)
    coarse = scale.astype(BF16)
    fine = (scale - coarse.astype(F32)).astype(BF16)
    pieces = jnp.concatenate([coarse.astype(F32), fine.astype(F32)], axis=0).astype(BF16)

    def scale_copy(d):
        return remote(
            scale_send.at[d], scale_recv.at[d], scale_s.at[d], scale_r.at[d], bank(d)
        )

    def slot_scales(d):
        found = lax.dot_general(
            pieces, pick[d], (((1,), (1,)), ((), ())), preferred_element_type=F32
        )
        scale_send[d, :1, :slots] = found[:1]
        scale_send[d, 1:, :slots] = found[8:9]

    def row_copy(d):
        return remote(
            stage.at[d], recv.at[d], row_s.at[d], row_r.at[d], bank(d)
        )

    def dispatch(d):
        stage[d] = dot(pick[d], keys[:, back]).astype(BF16)
        row_copy(d).start()

    def dispatch_scales(d):
        slot_scales(d)
        scale_copy(d).start()

    each(1, n, dispatch_scales)
    each(1, n, dispatch)
    stage[0] = dot(pick[0], keys[:, back]).astype(BF16)
    stage_lead[0] = dot(pick[0], keys[:, front]).astype(BF16)
    slot_scales(0)

    def matches(cluster_ids):
        return lax.broadcasted_iota(jnp.int32, (owned, slots), 0) == cluster_ids

    def lead_sum(found, scales, rows_in):
        return dot(jnp.where(found, scales[:1, :slots], 0.0).astype(BF16), rows_in) + dot(
            jnp.where(found, scales[1:, :slots], 0.0).astype(BF16), rows_in
        )

    found = matches(ids_send[0, :1, :slots])
    ones = jnp.where(found, 1.0, 0.0)
    counts[...] = jnp.broadcast_to(jnp.sum(ones, axis=1, keepdims=True), counts.shape)
    sums[:, back] = dot(ones.astype(BF16), stage[0])
    sums[:, front] = lead_sum(found, scale_send[0], stage_lead[0])

    def match(d):
        id_copy(d).wait()
        chosen = jnp.where(matches(ids_recv[d, :1, :slots]), 1.0, 0.0)
        member[d] = chosen.astype(BF16)
        counts[...] += jnp.sum(chosen, axis=1, keepdims=True)

    each(1, n, match)

    def collect_lead(d):
        lead_rows(d).wait()
        scale_copy(d).wait()
        found = matches(ids_recv[d, :1, :slots])
        sums[:, front] += lead_sum(found, scale_recv[d], recv_lead[d])

    each(1, n, collect_lead)
    loads[3].wait()

    def collect(d):
        row_copy(d).wait()
        sums[:, back] += dot(member[d], recv[d])

    each(1, n, collect)

    fin_copies = []
    for b in range(n_out):
        block = slice(b * out_block, (b + 1) * out_block)
        pooled = (sums[block, :] + old[block, :].astype(F32)) / (counts[block, :1] + 1.0)
        sums[block, :] = pooled
        fin_send[block, :] = jnp.broadcast_to(
            jnp.sum(pooled * pooled, axis=1, keepdims=True), (out_block, 128)
        )
        copy = remote(fin_send.at[block], fin_recv.at[block], fin_s.at[b], fin_r.at[b], other)
        copy.start()
        fin_copies.append(copy)
    half_copies = []
    for b in range(n_out):
        block = slice(b * out_block, (b + 1) * out_block)
        fin_copies[b].wait()
        total = fin_send[block, :1] + fin_recv[block, :1]
        fin_half[block, :] = (sums[block, :] * lax.rsqrt(total / D + epsilon)).astype(BF16)
        place_at = out_ref.at[block, mine]
        copy = remote(fin_half.at[block], place_at, half_s.at[b], half_r.at[b], other)
        copy.start()
        here = pltpu.make_async_copy(fin_half.at[block], place_at, own_s.at[b])
        here.start()
        half_copies += [copy, here]
    for copy in half_copies:
        copy.wait()


def shards(features, cluster_ids, w_in, w_out, old_centroids):
    n = lax.axis_size("bank")
    rows, half = features.shape
    hidden = w_in.shape[1]
    owned = old_centroids.shape[0]
    capacity = 3 * rows // n
    slots = -(-capacity // 16) * 16
    width = -(-slots // 128) * 128
    n_rows, n_out = 3, 4
    lead = 128
    vmem, dma = pltpu.VMEM, pltpu.SemaphoreType.DMA
    anywhere = pl.BlockSpec(memory_space=pl.ANY)
    far = pl.BlockSpec(memory_space=pltpu.HBM)
    return pl.pallas_call(
        functools.partial(kernel, n, n_rows, n_out),
        out_shape=jax.ShapeDtypeStruct((owned, 2 * half), BF16),
        in_specs=[
            far, pl.BlockSpec(memory_space=pltpu.VMEM), far, far, far,
        ],
        out_specs=anywhere,
        scratch_shapes=[
            vmem((rows, half), BF16),
            vmem((rows, half), BF16),
            vmem(w_in.shape, BF16),
            vmem(w_out.shape, BF16),
            vmem((owned, half), BF16),
            vmem((rows, hidden), F32),
            vmem((rows, hidden), BF16),
            vmem((rows, half), F32),
            vmem((rows, half), F32),
            vmem((rows, half), F32),
            vmem((8, rows), F32),
            vmem((8, rows), F32),
            vmem((rows, half), BF16),
            vmem((n, slots, rows), BF16),
            vmem((n, slots, lead), BF16),
            vmem((n, slots, lead), BF16),
            vmem((n, slots, half - lead), BF16),
            vmem((n, slots, half - lead), BF16),
            vmem((n, 8, width), jnp.int32),
            vmem((n, 8, width), jnp.int32),
            vmem((n, owned, slots), BF16),
            vmem((owned, 128), F32),
            vmem((owned, half), F32),
            vmem((n, 2, width), F32),
            vmem((n, 2, width), F32),
            vmem((owned, 128), F32),
            vmem((owned, 128), F32),
            vmem((owned, half), BF16),
            dma((4,)), dma, dma, dma((n_rows + 1,)), dma((n_rows + 1,)), dma, dma,
            dma((n,)), dma((n,)), dma((n,)), dma((n,)), dma((n,)), dma((n,)), dma((n,)), dma((n,)),
            dma((n_out,)), dma((n_out,)), dma((n_out,)), dma((n_out,)), dma((n_out,)),
        ],
        compiler_params=pltpu.CompilerParams(
            collective_id=0, has_side_effects=True, vmem_limit_bytes=50 * 1024 * 1024
        ),
    )(
        pltpu.with_memory_space_constraint(features, pltpu.HBM),
        cluster_ids,
        pltpu.with_memory_space_constraint(w_in, pltpu.HBM),
        pltpu.with_memory_space_constraint(w_out, pltpu.HBM),
        pltpu.with_memory_space_constraint(old_centroids, pltpu.HBM),
    )


def solution(mesh):
    placed = (
        P(("groups", "bank"), "clus"),
        P(("groups", "bank")),
        P(None, "clus"),
        P("clus", None),
        P(("groups", "bank"), "clus"),
    )
    return jax.shard_map(
        shards, mesh=mesh, in_specs=placed, out_specs=P(("groups", "bank"), None), check_vma=False
    )
```

```python
import functools

import jax
import jax.numpy as jnp
from jax import lax
from jax.experimental import pallas as pl
from jax.experimental.pallas import tpu as pltpu
from jax.sharding import PartitionSpec as P

D = 768
epsilon = 1e-06
BF16 = jnp.bfloat16
F32 = jnp.float32
MESH = pl.DeviceIdType.MESH


def dot(a, b):
    return jnp.dot(a, b, preferred_element_type=F32)


def each(low, high, body):
    if high - low <= 8:
        for d in range(low, high):
            body(d)
    else:

        def step(d, carry):
            body(d)
            return carry

        lax.fori_loop(low, high, step, 0)


def kernel(
    n, n_rows, n_out, features_in, ids_ref, w_in_in, w_out_in, old_in, out_ref,
    features, peer, w_in, w_out, old, hidden_sum, hidden, part, part_send, part_recv,
    sq_send, sq_recv, keys, pick, stage_lead, recv_lead, stage, recv, ids_send, ids_recv, member, counts, sums, scale_send, scale_recv,
    fin_send, fin_recv, fin_half, load_sems, pair_send, pair_recv, part_s, part_r,
    sq_s, sq_r, ids_s, ids_r, lead_s, lead_r, scale_s, scale_r, row_s, row_r, fin_s, fin_r, half_s, half_r, own_s,
):
    group = lax.axis_index("groups")
    me = lax.axis_index("bank")
    core = lax.axis_index("clus")
    rows, half = features.shape
    owned = sums.shape[0]
    slots = recv.shape[1]
    row_block = rows // n_rows
    out_block = owned // n_out
    other = (group, me, 1 - core)

    def bank(d):
        return (group, lax.rem(me + d, n), core)

    def remote(src, dst, send, arrive, to):
        return pltpu.make_async_remote_copy(
            src_ref=src, dst_ref=dst, send_sem=send, recv_sem=arrive,
            device_id=to, device_id_type=MESH,
        )

    barrier = pltpu.get_barrier_semaphore()
    pl.semaphore_signal(barrier, inc=1, device_id=other, device_id_type=MESH)
    each(
        1, n,
        lambda d: pl.semaphore_signal(barrier, inc=1, device_id=bank(d), device_id_type=MESH),
    )
    loads = [
        pltpu.make_async_copy(src, dst, load_sems.at[i])
        for i, (src, dst) in enumerate(
            ((features_in, features), (w_in_in, w_in), (w_out_in, w_out), (old_in, old))
        )
    ]
    for load in loads:
        load.start()

    ids = ids_ref[...].reshape(1, rows)
    owner = lax.div(ids, jnp.int32(owned))
    local = ids - owner * owned + 1
    owner_rows = max(16, n)
    table = jnp.where(
        lax.broadcasted_iota(jnp.int32, (owner_rows, rows), 0) == owner, 1.0, 0.0
    )
    earlier = jnp.where(
        lax.broadcasted_iota(jnp.int32, (rows, rows), 0)
        < lax.broadcasted_iota(jnp.int32, (rows, rows), 1),
        1.0, 0.0,
    ).astype(BF16)
    before = dot(table.astype(BF16), earlier)
    rank = jnp.sum(before * table, axis=0, keepdims=True).astype(jnp.int32)
    high = lax.div(local, jnp.int32(32))
    low = local - 32 * high
    digits = jnp.where(
        lax.broadcasted_iota(jnp.int32, (16, rows), 0) < 8, high, low
    ).astype(F32).astype(BF16)

    def place(d):
        to = lax.rem(me + d, n)
        slot = jnp.where(owner == to, rank, -1)
        chosen = jnp.where(
            lax.broadcasted_iota(jnp.int32, (slots, rows), 0) == slot, 1.0, 0.0
        ).astype(BF16)
        pick[d] = chosen
        found = lax.dot_general(
            digits, chosen, (((1,), (1,)), ((), ())), preferred_element_type=F32
        )
        ids_send[d, :, :slots] = (32.0 * found[:8] + found[8:] - 1.0).astype(jnp.int32)

    each(0, n, place)

    pl.semaphore_wait(barrier, n)
    loads[0].wait()
    to_peer = []
    for b in range(n_rows):
        block = slice(b * row_block, (b + 1) * row_block)
        copy = remote(features.at[block], peer.at[block], pair_send.at[b], pair_recv.at[b], other)
        copy.start()
        to_peer.append(copy)

    def id_copy(d):
        return remote(ids_send.at[d], ids_recv.at[d], ids_s.at[d], ids_r.at[d], bank(d))

    each(1, n, lambda d: id_copy(d).start())

    mine = pl.ds(pl.multiple_of(core * half, 128), half)
    theirs = pl.ds(pl.multiple_of((1 - core) * half, 128), half)
    loads[1].wait()
    hidden_sum[...] = dot(features[...], w_in[mine, :])
    loads[2].wait()
    lead = recv_lead.shape[2]
    front, back = slice(0, lead), slice(lead, half)

    def columns(first, width, own):
        base = core if own else 1 - core
        return pl.ds(pl.multiple_of(base * half + first, 128), width)

    lead_copies = []
    for b in range(n_rows):
        block = slice(b * row_block, (b + 1) * row_block)
        to_peer[b].wait()
        hidden[block, :] = jax.nn.gelu(
            hidden_sum[block, :] + dot(peer[block, :], w_in[theirs, :])
        ).astype(BF16)
        part_send[block, front] = dot(hidden[block, :], w_out[:, columns(0, lead, False)])
        copy = remote(
            part_send.at[block, front], part_recv.at[block, front],
            part_s.at[b], part_r.at[b], other,
        )
        copy.start()
        lead_copies.append(copy)
    part_send[:, back] = dot(hidden[...], w_out[:, columns(lead, half - lead, False)])
    rest_copy = remote(
        part_send.at[:, back], part_recv.at[:, back],
        part_s.at[n_rows], part_r.at[n_rows], other,
    )
    rest_copy.start()
    part[:, front] = features[:, front].astype(F32) + dot(
        hidden[...], w_out[:, columns(0, lead, True)]
    )
    for copy in lead_copies:
        copy.wait()
    lead_residual = part[:, front] + part_recv[:, front]
    keys[:, front] = lead_residual.astype(BF16)

    def lead_rows(d):
        return remote(
            stage_lead.at[d], recv_lead.at[d], lead_s.at[d], lead_r.at[d], bank(d)
        )

    def dispatch_lead(d):
        stage_lead[d] = dot(pick[d], keys[:, front]).astype(BF16)
        lead_rows(d).start()

    each(1, n, dispatch_lead)

    part[:, back] = features[:, back].astype(F32) + dot(
        hidden[...], w_out[:, columns(lead, half - lead, True)]
    )
    lead_squares = jnp.sum(lead_residual * lead_residual, axis=1, keepdims=True)
    rest_copy.wait()
    residual = part[:, back] + part_recv[:, back]
    part[:, back] = residual
    squares = lead_squares + jnp.sum(residual * residual, axis=1, keepdims=True)
    sq_send[...] = jnp.transpose(jnp.broadcast_to(squares, (rows, 128)))[:8]
    sq_copy = remote(sq_send, sq_recv, sq_s, sq_r, other)
    sq_copy.start()
    sq_copy.wait()
    scale = lax.rsqrt((sq_send[...] + sq_recv[...]) / D + epsilon)
    column = jnp.transpose(jnp.broadcast_to(scale[:1], (128, rows)))[:, :1]
    keys[:, back] = (part[:, back] * column).astype(BF16)
    coarse = scale.astype(BF16)
    fine = (scale - coarse.astype(F32)).astype(BF16)
    pieces = jnp.concatenate([coarse.astype(F32), fine.astype(F32)], axis=0).astype(BF16)

    def scale_copy(d):
        return remote(
            scale_send.at[d], scale_recv.at[d], scale_s.at[d], scale_r.at[d], bank(d)
        )

    def slot_scales(d):
        found = lax.dot_general(
            pieces, pick[d], (((1,), (1,)), ((), ())), preferred_element_type=F32
        )
        scale_send[d, :1, :slots] = found[:1]
        scale_send[d, 1:, :slots] = found[8:9]

    def row_copy(d):
        return remote(
            stage.at[d], recv.at[d], row_s.at[d], row_r.at[d], bank(d)
        )

    def dispatch(d):
        stage[d] = dot(pick[d], keys[:, back]).astype(BF16)
        row_copy(d).start()

    def dispatch_scales(d):
        slot_scales(d)
        scale_copy(d).start()

    each(1, n, dispatch_scales)
    each(1, n, dispatch)
    stage[0] = dot(pick[0], keys[:, back]).astype(BF16)
    stage_lead[0] = dot(pick[0], keys[:, front]).astype(BF16)
    slot_scales(0)

    def matches(cluster_ids):
        return lax.broadcasted_iota(jnp.int32, (owned, slots), 0) == cluster_ids

    def lead_sum(found, scales, rows_in):
        return dot(jnp.where(found, scales[:1, :slots], 0.0).astype(BF16), rows_in) + dot(
            jnp.where(found, scales[1:, :slots], 0.0).astype(BF16), rows_in
        )

    found = matches(ids_send[0, :1, :slots])
    ones = jnp.where(found, 1.0, 0.0)
    counts[...] = jnp.broadcast_to(jnp.sum(ones, axis=1, keepdims=True), counts.shape)
    sums[:, back] = dot(ones.astype(BF16), stage[0])
    sums[:, front] = lead_sum(found, scale_send[0], stage_lead[0])

    def match(d):
        id_copy(d).wait()
        chosen = jnp.where(matches(ids_recv[d, :1, :slots]), 1.0, 0.0)
        member[d] = chosen.astype(BF16)
        counts[...] += jnp.sum(chosen, axis=1, keepdims=True)

    each(1, n, match)

    def collect_lead(d):
        lead_rows(d).wait()
        scale_copy(d).wait()
        found = matches(ids_recv[d, :1, :slots])
        sums[:, front] += lead_sum(found, scale_recv[d], recv_lead[d])

    each(1, n, collect_lead)
    loads[3].wait()

    def collect(d):
        row_copy(d).wait()
        sums[:, back] += dot(member[d], recv[d])

    each(1, n, collect)

    fin_copies = []
    for b in range(n_out):
        block = slice(b * out_block, (b + 1) * out_block)
        pooled = (sums[block, :] + old[block, :].astype(F32)) / (counts[block, :1] + 1.0)
        sums[block, :] = pooled
        fin_send[block, :] = jnp.broadcast_to(
            jnp.sum(pooled * pooled, axis=1, keepdims=True), (out_block, 128)
        )
        copy = remote(fin_send.at[block], fin_recv.at[block], fin_s.at[b], fin_r.at[b], other)
        copy.start()
        fin_copies.append(copy)
    half_copies = []
    for b in range(n_out):
        block = slice(b * out_block, (b + 1) * out_block)
        fin_copies[b].wait()
        total = fin_send[block, :1] + fin_recv[block, :1]
        fin_half[block, :] = (sums[block, :] * lax.rsqrt(total / D + epsilon)).astype(BF16)
        place_at = out_ref.at[block, mine]
        copy = remote(fin_half.at[block], place_at, half_s.at[b], half_r.at[b], other)
        copy.start()
        here = pltpu.make_async_copy(fin_half.at[block], place_at, own_s.at[b])
        here.start()
        half_copies += [copy, here]
    for copy in half_copies:
        copy.wait()


def shards(features, cluster_ids, w_in, w_out, old_centroids):
    n = lax.axis_size("bank")
    rows, half = features.shape
    hidden = w_in.shape[1]
    owned = old_centroids.shape[0]
    capacity = 3 * rows // n
    slots = -(-capacity // 16) * 16
    width = -(-slots // 128) * 128
    n_rows, n_out = 3, 4
    lead = 128
    vmem, dma = pltpu.VMEM, pltpu.SemaphoreType.DMA
    anywhere = pl.BlockSpec(memory_space=pl.ANY)
    far = pl.BlockSpec(memory_space=pltpu.HBM)
    return pl.pallas_call(
        functools.partial(kernel, n, n_rows, n_out),
        out_shape=jax.ShapeDtypeStruct((owned, 2 * half), BF16),
        in_specs=[
            far, pl.BlockSpec(memory_space=pltpu.VMEM), far, far, far,
        ],
        out_specs=anywhere,
        scratch_shapes=[
            vmem((rows, half), BF16),
            vmem((rows, half), BF16),
            vmem(w_in.shape, BF16),
            vmem(w_out.shape, BF16),
            vmem((owned, half), BF16),
            vmem((rows, hidden), F32),
            vmem((rows, hidden), BF16),
            vmem((rows, half), F32),
            vmem((rows, half), F32),
            vmem((rows, half), F32),
            vmem((8, rows), F32),
            vmem((8, rows), F32),
            vmem((rows, half), BF16),
            vmem((n, slots, rows), BF16),
            vmem((n, slots, lead), BF16),
            vmem((n, slots, lead), BF16),
            vmem((n, slots, half - lead), BF16),
            vmem((n, slots, half - lead), BF16),
            vmem((n, 8, width), jnp.int32),
            vmem((n, 8, width), jnp.int32),
            vmem((n, owned, slots), BF16),
            vmem((owned, 128), F32),
            vmem((owned, half), F32),
            vmem((n, 2, width), F32),
            vmem((n, 2, width), F32),
            vmem((owned, 128), F32),
            vmem((owned, 128), F32),
            vmem((owned, half), BF16),
            dma((4,)), dma((n_rows,)), dma((n_rows,)), dma((n_rows + 1,)), dma((n_rows + 1,)), dma, dma,
            dma((n,)), dma((n,)), dma((n,)), dma((n,)), dma((n,)), dma((n,)), dma((n,)), dma((n,)),
            dma((n_out,)), dma((n_out,)), dma((n_out,)), dma((n_out,)), dma((n_out,)),
        ],
        compiler_params=pltpu.CompilerParams(
            collective_id=0, has_side_effects=True, vmem_limit_bytes=50 * 1024 * 1024
        ),
    )(
        pltpu.with_memory_space_constraint(features, pltpu.HBM),
        cluster_ids,
        pltpu.with_memory_space_constraint(w_in, pltpu.HBM),
        pltpu.with_memory_space_constraint(w_out, pltpu.HBM),
        pltpu.with_memory_space_constraint(old_centroids, pltpu.HBM),
    )


def solution(mesh):
    placed = (
        P(("groups", "bank"), "clus"),
        P(("groups", "bank")),
        P(None, "clus"),
        P("clus", None),
        P(("groups", "bank"), "clus"),
    )
    return jax.shard_map(
        shards, mesh=mesh, in_specs=placed, out_specs=P(("groups", "bank"), None), check_vma=False
    )
```
